32 devices in a mesh: dp: 4 (over y, x), mp: 8 (over z, core).
Axes of the slice: x: 2, y: 2, z: 4, core: 2. Of those that a mesh axis runs over, the one named last changes fastest.
Arguments:
- features: bfloat16 [1024, 8192], P('dp', 'mp'), may hold values from -6 to 6
- out_grads: bfloat16 [1024, 8192], P('dp', 'mp'), may hold values from -0.5 to 0.5
- matching: int32 [2, 8], P(None, 'mp'), may hold values 0 or 1
Outputs:
- blocks: bfloat16 [8192, 8192], P('dp', 'mp')
The draws below stay inside these ranges and needn't reach their ends.
All inputs are finite; a program needn't handle non-finite values. No bound on the sum of `matching` on one device may be relied on, other than what follows from the above.
Results may differ from the reference program's by a relative error of at most 0.006.
Values may be sent and summed in bfloat16 or wider, within the bound.
A program may use at most 128 MiB of HBM per device.

```python
import jax
import jax.numpy as jnp
from jax import lax

D = 8192
BLOCK = 512
ROUNDS = 2
NS_STEPS = 2
COLS = 8192
TOKENS = 1024
N_MP = 8


def touch_ends(result, stream_key, least, top_value):
    extent = result.shape
    spot = [jax.random.randint(jax.random.fold_in(stream_key, axis), (), 0, extent[axis]) for axis in range(len(extent))]
    result = result.at[tuple(spot)].set(least)
    longest = extent.index(max(extent))
    spot[longest] = (spot[longest] + 1) % extent[longest]
    return result.at[tuple(spot)].set(top_value)


def level_of(stream_key, extent, cuts, smallest, top_value):
    def one(axis_at, parts):
        draws = jax.random.uniform(jax.random.fold_in(jax.random.fold_in(stream_key, 6), axis_at), (parts,), jnp.float32, smallest / len(cuts), top_value / len(cuts))
        return jnp.repeat(jnp.exp(draws), extent[axis_at] // parts).reshape((-1,) + (1,) * (len(extent) - axis_at - 1))

    factor_of = one(*cuts[0])
    for cut in cuts[1:]:
        factor_of = factor_of * one(*cut)
    return factor_of


def centred(key, dims, deviation, limit, pieces=(), kind=jnp.bfloat16):
    result = jax.random.normal(key, dims, jnp.float32) * deviation
    if len(pieces) > 0:
        result = level_of(key, dims, pieces, -0.22, 0.18) * result
    return jnp.clip(result, min=-limit, max=limit).astype(kind)


def setup_inputs(seed: int = 0) -> dict:
    key_of = jax.random.split(jax.random.key(seed), 4)
    return {
        "features": centred(key_of[0], (TOKENS, D), 1.0, 6.0, ((0, 4), (1, 8))),
        "out_grads": centred(key_of[1], (TOKENS, COLS), (TOKENS ** -0.5), 0.5, ((0, 4), (1, 8))),
        "matching": touch_ends((jax.random.randint(key_of[2], (ROUNDS, N_MP), 0, 2) < 1).astype(jnp.int32), jax.random.fold_in(key_of[2], 1), 0, 1),
    }


def contract_rows(left, right):
    return lax.dot_general(left.astype(jnp.float32), right.astype(jnp.float32), (((0,), (0,)), ((), ())))

def polar_factor(cross):
    width = cross.shape[0]
    scale = 0.5 * lax.rsqrt(jnp.sum(cross * cross) + 1e-06)
    zeros = jnp.zeros((width, width), jnp.float32)
    upper = jnp.concatenate([zeros, scale * cross], axis=1)
    lower = jnp.concatenate([-scale * cross.T, zeros], axis=1)
    iterate = (jnp.eye(2 * width, dtype=jnp.float32) + jnp.concatenate([upper, lower], axis=0)).astype(jnp.bfloat16)
    for step in range(NS_STEPS):
        product = lax.dot_general(iterate, iterate, (((1,), (1,)), ((), ())), preferred_element_type=jnp.float32).astype(jnp.bfloat16)
        cubic = jnp.dot(product, iterate, preferred_element_type=jnp.float32)
        iterate = (1.5 * iterate.astype(jnp.float32) - 0.5 * cubic).astype(jnp.bfloat16)
    return iterate

def one_pair(pair_args):
    first, second = pair_args
    cross = jnp.dot(first.T, second, preferred_element_type=jnp.float32)
    rotation = polar_factor(cross)
    joined = jnp.concatenate([first, second], axis=1)
    turned = jnp.dot(joined, rotation, preferred_element_type=jnp.float32).astype(jnp.bfloat16)
    return (turned[:, :BLOCK], turned[:, BLOCK:])

def reference(features, out_grads, matching):
    grad = jnp.dot(features.T, out_grads, preferred_element_type=jnp.float32).astype(jnp.bfloat16)
    split_cols = grad.reshape(D, N_MP, 2, BLOCK)
    first = jnp.transpose(split_cols[:, :, 0, :], (1, 0, 2))
    second = jnp.transpose(split_cols[:, :, 1, :], (1, 0, 2))
    for step in range(ROUNDS):
        first, second = lax.map(one_pair, (first, second))
        picks = matching[step][:, None, None]
        moving = jnp.where(picks == 0, second, first)
        staying = jnp.where(picks == 0, first, second)
        first = staying
        second = jnp.roll(moving, 1, axis=0)
    stacked = jnp.stack([first, second], axis=2)
    return jnp.transpose(stacked, (1, 0, 2, 3)).reshape(D, 2 * BLOCK * N_MP)
```

```python
import jax
import jax.numpy as jnp
from jax import lax
from jax.sharding import PartitionSpec as P

ROUNDS = 2


def shifted(value, axis, steps):
    count = lax.axis_size(axis)
    pairs = [(source, (source + steps) % count) for source in range(count)]
    return lax.ppermute(value, axis, pairs)


def dot(left, right, left_dim=1, right_dim=0):
    return lax.dot_general(
        left, right, (((left_dim,), (right_dim,)), ((), ())), preferred_element_type=jnp.float32
    )


def low(value):
    return value.astype(jnp.bfloat16)


def even_part(square):
    width = square.shape[0]
    half = low(square)
    second = dot(half, half)
    tail = 0.375 * jnp.eye(width, dtype=jnp.float32) - 0.3125 * square + 0.0625 * second
    return -0.5 * square + dot(low(second), low(tail))


def rotation_less_one(cross):
    scale = 0.5 * lax.rsqrt(jnp.sum(cross * cross) + 1e-06)
    angle = low(scale * cross)
    upper = even_part(dot(angle, angle, 1, 1))
    lower = even_part(dot(angle, angle, 0, 0))
    upper = low(upper)
    side = low(angle.astype(jnp.float32) + dot(upper, angle))
    return jnp.concatenate(
        [
            jnp.concatenate([upper, side], axis=1),
            jnp.concatenate([-side.T, low(lower)], axis=1),
        ],
        axis=0,
    )


def on_device(features, out_grads, matching):
    width = out_grads.shape[1] // 2
    column = lax.all_gather(features, "dp", axis=0, tiled=True)
    joined = lax.all_gather(out_grads, "dp", axis=0, tiled=True)
    wide = lax.all_gather(features, "mp", axis=1, tiled=True)
    rows = lax.all_to_all(wide, "dp", split_axis=1, concat_axis=0, tiled=True)
    slab = lax.psum_scatter(dot(features, column, 1, 1), "mp", scatter_dimension=0, tiled=True)
    gram = lax.all_gather(low(slab), ("dp", "mp"), axis=0, tiled=True)
    for step in range(ROUNDS):
        first = joined[:, :width]
        second = joined[:, width:]
        cross = dot(first, low(dot(gram, second)), 0, 0)
        turned = low(joined.astype(jnp.float32) + dot(joined, rotation_less_one(cross)))
        first = turned[:, :width]
        second = turned[:, width:]
        picked = matching[step, 0]
        moving = jnp.where(picked == 0, second, first)
        staying = jnp.where(picked == 0, first, second)
        arrived = shifted(moving, "mp", 1)
        joined = jnp.concatenate([staying, arrived], axis=1)
    return low(dot(rows, joined, 0, 0))


def solution(mesh):
    return jax.shard_map(
        on_device,
        mesh=mesh,
        in_specs=(P("dp", "mp"), P("dp", "mp"), P(None, "mp")),
        out_specs=P("dp", "mp"),
        check_vma=False,
    )
```

```python
import functools

import jax
import jax.numpy as jnp
from jax import lax
from jax.experimental import pallas as pl
from jax.experimental.pallas import tpu as pltpu
from jax.sharding import PartitionSpec as P

ROUNDS = 2
TILE = 256
VMEM_BYTES = 44 * 1024 * 1024
MESH = pl.DeviceIdType.MESH


def shifted(value, axis, steps):
    count = lax.axis_size(axis)
    pairs = [(source, (source + steps) % count) for source in range(count)]
    return lax.ppermute(value, axis, pairs)


def dot(left, right, left_dim=1, right_dim=0):
    return lax.dot_general(
        left, right, (((left_dim,), (right_dim,)), ((), ())), preferred_element_type=jnp.float32
    )


def low(value):
    return value.astype(jnp.bfloat16)


def gram_kernel(
    n_dp, n_chips, f_ref, o_ref, all_ref, gram_ref,
    others, slab, sibling_half, out_half, chip_in,
    f_send, f_recv, o_send, o_recv, s_send, s_recv, z_send, z_recv,
    a_send, a_recv, b_send, b_recv, c_send, c_recv,
):
    tokens = f_ref.shape[0]
    half = tokens // 2
    piece = half // n_chips
    row = lax.axis_index("dp")
    owner = lax.axis_index("mp")
    chip = owner // 2
    core = owner % 2
    sibling = {"dp": row, "mp": chip * 2 + (1 - core)}
    rows = [{"dp": lax.rem(row + s, n_dp), "mp": owner} for s in range(1, n_dp)]
    chips = [{"dp": row, "mp": lax.rem(chip + s, n_chips) * 2 + core} for s in range(1, n_chips)]

    def remote(source, target, send, recv, device):
        return pltpu.make_async_remote_copy(
            src_ref=source, dst_ref=target, send_sem=send, recv_sem=recv,
            device_id=device, device_id_type=MESH,
        )

    barrier = pltpu.get_barrier_semaphore()
    for device in rows + chips + [sibling]:
        pl.semaphore_signal(barrier, inc=1, device_id=device, device_id_type=MESH)
    pl.semaphore_wait(barrier, n_dp + n_chips - 1)

    f_copies = [
        remote(f_ref, others.at[s], f_send.at[s], f_recv.at[s], rows[s]) for s in range(n_dp - 1)
    ]
    own_tokens = pl.ds(pl.multiple_of(row * tokens, tokens), tokens)
    o_copies = [
        remote(o_ref, all_ref.at[own_tokens], o_send.at[s], o_recv.at[s], rows[s])
        for s in range(n_dp - 1)
    ]
    for copy in f_copies + o_copies:
        copy.start()
    all_ref[own_tokens, :] = o_ref[...]

    slab[:, own_tokens] = dot(f_ref[...], f_ref[...], 1, 1)
    for s in range(n_dp - 1):
        source = lax.rem(row + n_dp - s - 1, n_dp)
        f_copies[s].wait_recv()
        slab[:, pl.ds(pl.multiple_of(source * tokens, tokens), tokens)] = dot(
            f_ref[...], others[s], 1, 1
        )

    theirs = pl.ds(pl.multiple_of((1 - core) * half, half), half)
    to_sibling = remote(slab.at[theirs], sibling_half, s_send, s_recv, sibling)
    to_sibling.start()
    to_sibling.wait_recv()
    mine = pl.multiple_of(core * half, half)
    out_half[...] = low(slab[pl.ds(mine, half), :] + sibling_half[...])

    z_copies = []
    for s in range(n_chips - 1):
        target = lax.rem(chip + s + 1, n_chips)
        z_copies.append(
            remote(
                out_half.at[pl.ds(pl.multiple_of(target * piece, piece), piece)],
                chip_in.at[s], z_send.at[s], z_recv.at[s], chips[s],
            )
        )
        z_copies[-1].start()
    offset = pl.multiple_of(chip * piece, piece)
    total = slab[pl.ds(pl.multiple_of(mine + offset, piece), piece), :] + sibling_half[pl.ds(offset, piece), :]
    for s in range(n_chips - 1):
        z_copies[s].wait_recv()
        total = total + chip_in[s].astype(jnp.float32)

    start = row * tokens + mine
    block = pl.ds(pl.multiple_of(start + offset, piece), piece)
    gram_ref[block, :] = low(total)
    a_copies = [
        remote(gram_ref.at[block], gram_ref.at[block], a_send.at[s], a_recv.at[s], chips[s])
        for s in range(n_chips - 1)
    ]
    for copy in a_copies:
        copy.start()
    for copy in a_copies:
        copy.wait_recv()

    strip = pl.ds(pl.multiple_of(start, half), half)
    b_copies = [
        remote(gram_ref.at[strip], gram_ref.at[strip], b_send.at[s], b_recv.at[s], rows[s])
        for s in range(n_dp - 1)
    ]
    for copy in b_copies:
        copy.start()
    c_copies = [remote(gram_ref.at[strip], gram_ref.at[strip], c_send.at[0], c_recv.at[0], sibling)]
    c_copies[0].start()
    for s in range(n_dp - 1):
        source = lax.rem(row + n_dp - s - 1, n_dp)
        b_copies[s].wait_recv()
        arrived = pl.ds(pl.multiple_of(source * tokens + mine, half), half)
        c_copies.append(
            remote(gram_ref.at[arrived], gram_ref.at[arrived], c_send.at[s + 1], c_recv.at[s + 1], sibling)
        )
        c_copies[-1].start()
    for copy in c_copies + o_copies:
        copy.wait_recv()
    for copy in f_copies + o_copies + [to_sibling] + z_copies + a_copies + b_copies + c_copies:
        copy.wait_send()


def gather_and_gram(features, out_grads, n_dp, n_mp):
    tokens, depth = features.shape
    every = n_dp * tokens
    n_chips = n_mp // 2
    half = tokens // 2
    dma = pltpu.SemaphoreType.DMA
    peers = [dma((n_dp - 1,))] * 2
    around = [dma((n_chips - 1,))] * 2
    whole = pl.BlockSpec(memory_space=pltpu.VMEM)
    return pl.pallas_call(
        functools.partial(gram_kernel, n_dp, n_chips),
        out_shape=[
            jax.ShapeDtypeStruct((every, out_grads.shape[1]), jnp.bfloat16),
            jax.ShapeDtypeStruct((every, every), jnp.bfloat16),
        ],
        in_specs=[whole, whole],
        out_specs=[whole, whole],
        scratch_shapes=[
            pltpu.VMEM((n_dp - 1, tokens, depth), jnp.bfloat16),
            pltpu.VMEM((tokens, every), jnp.float32),
            pltpu.VMEM((half, every), jnp.float32),
            pltpu.VMEM((half, every), jnp.bfloat16),
            pltpu.VMEM((n_chips - 1, half // n_chips, every), jnp.bfloat16),
        ]
        + peers + peers + [dma, dma] + around + around + peers + [dma((n_dp,))] * 2,
        compiler_params=pltpu.CompilerParams(
            collective_id=0, has_side_effects=True, vmem_limit_bytes=VMEM_BYTES
        ),
        cost_estimate=pl.CostEstimate(flops=2 * tokens * every * depth, bytes_accessed=200_000_000, transcendentals=0),
        name="gather_and_gram",
    )(features, out_grads)


def even_part(square):
    width = square.shape[0]
    half = low(square)
    second = dot(half, half)
    on_diagonal = lax.broadcasted_iota(jnp.int32, (width, width), 0) == lax.broadcasted_iota(
        jnp.int32, (width, width), 1
    )
    tail = jnp.where(on_diagonal, 0.375, 0.0) - 0.3125 * square + 0.0625 * second
    return low(-0.5 * square + dot(low(second), low(tail)))


def round_kernel(picked_ref, gram_ref, first_ref, second_ref, staying_ref, moving_ref, cross, upper, lower, side):
    tokens = gram_ref.shape[0]
    cross[...] = jnp.zeros_like(cross)

    @pl.loop(0, tokens // TILE)
    def _(step):
        tile = pl.ds(pl.multiple_of(step * TILE, TILE), TILE)
        cross[...] += dot(first_ref[tile, :], low(dot(gram_ref[tile, :], second_ref[...])), 0, 0)

    value = cross[...]
    scale = 0.5 * lax.rsqrt(jnp.sum(value * value) + 1e-06)
    angle = low(scale * value)
    upper[...] = even_part(dot(angle, angle, 1, 1))
    lower[...] = even_part(dot(angle, angle, 0, 0))
    side[...] = low(angle.astype(jnp.float32) + dot(upper[...], angle))
    keep = picked_ref[0] == 0

    @pl.loop(0, tokens // TILE)
    def _(step):
        tile = pl.ds(pl.multiple_of(step * TILE, TILE), TILE)
        first = first_ref[tile, :]
        second = second_ref[tile, :]
        new_first = low(first.astype(jnp.float32) + (dot(first, upper[...]) - dot(second, side[...], 1, 1)))
        new_second = low(second.astype(jnp.float32) + (dot(first, side[...]) + dot(second, lower[...])))
        moving_ref[tile, :] = jnp.where(keep, new_second, new_first)
        staying_ref[tile, :] = jnp.where(keep, new_first, new_second)


def one_round(picked, gram, first, second, second_at):
    tokens = gram.shape[0]
    width = second.shape[1] // (second_at + 1)
    block = jax.ShapeDtypeStruct((tokens, width), jnp.bfloat16)
    return pl.pallas_call(
        round_kernel,
        grid=(1,),
        out_shape=[block, block],
        in_specs=[
            pl.BlockSpec(memory_space=pltpu.SMEM),
            pl.BlockSpec((tokens, tokens), lambda i: (0, 0)),
            pl.BlockSpec((tokens, width), lambda i: (0, 0)),
            pl.BlockSpec((tokens, width), lambda i: (0, second_at)),
        ],
        out_specs=[pl.BlockSpec((tokens, width), lambda i: (0, 0))] * 2,
        scratch_shapes=[
            pltpu.VMEM((width, width), jnp.float32),
            pltpu.VMEM((width, width), jnp.bfloat16),
            pltpu.VMEM((width, width), jnp.bfloat16),
            pltpu.VMEM((width, width), jnp.bfloat16),
        ],
        compiler_params=pltpu.CompilerParams(vmem_limit_bytes=VMEM_BYTES),
        cost_estimate=pl.CostEstimate(
            flops=2 * tokens * width * (tokens + 5 * width) + 14 * width**3,
            bytes_accessed=2 * tokens * (tokens + 4 * width), transcendentals=1,
        ),
        name="jacobi_round",
    )(picked, gram, first, second)


def product_kernel(n_dp, tokens, *refs):
    parts = refs[:n_dp]
    staying_ref, arrived_ref, out_ref = refs[n_dp:]
    row = lax.axis_index("dp")
    width = staying_ref.shape[1]
    for side, block in enumerate((staying_ref, arrived_ref)):
        total = None
        for s in range(n_dp):
            source = lax.rem(row + n_dp - s, n_dp)
            term = dot(parts[s][0], block[pl.ds(pl.multiple_of(source * tokens, tokens), tokens), :], 0, 0)
            total = term if total is None else total + term
        out_ref[:, side * width : (side + 1) * width] = low(total)


def final_product(parts, staying, arrived):
    n_dp = len(parts)
    groups, tokens, depth = parts[0].shape
    tile = min(TILE, depth)
    per = depth // tile
    width = staying.shape[1]
    full = pl.BlockSpec(staying.shape, lambda i: (0, 0))
    return pl.pallas_call(
        functools.partial(product_kernel, n_dp, tokens),
        grid=(groups * per,),
        out_shape=jax.ShapeDtypeStruct((groups * depth, 2 * width), jnp.bfloat16),
        in_specs=[pl.BlockSpec((1, tokens, tile), lambda i: (i // per, 0, i % per))] * n_dp + [full, full],
        out_specs=pl.BlockSpec((tile, 2 * width), lambda i: (i, 0)),
        compiler_params=pltpu.CompilerParams(vmem_limit_bytes=VMEM_BYTES),
        cost_estimate=pl.CostEstimate(
            flops=4 * groups * depth * width * tokens * n_dp,
            bytes_accessed=2 * groups * depth * (n_dp * tokens + 2 * width), transcendentals=0,
        ),
        name="final_product",
    )(*parts, staying, arrived)


def on_device(features, out_grads, matching):
    n_dp = lax.axis_size("dp")
    n_mp = lax.axis_size("mp")
    groups = n_mp // n_dp
    row = lax.axis_index("dp")
    wide = lax.all_gather(features, "mp", axis=0)
    joined, gram = gather_and_gram(features, out_grads, n_dp, n_mp)
    parts = []
    for s in range(n_dp):
        target = lax.rem(row + s, n_dp)
        part = lax.dynamic_slice_in_dim(wide, target * groups, groups, axis=0)
        parts.append(shifted(part, "dp", s) if s else part)
    first, second, second_at = joined, joined, 1
    for step in range(ROUNDS):
        first, moving = one_round(matching[step], gram, first, second, second_at)
        second, second_at = shifted(moving, "mp", 1), 0
    return final_product(parts, first, second)


def solution(mesh):
    return jax.shard_map(
        on_device,
        mesh=mesh,
        in_specs=(P("dp", "mp"), P("dp", "mp"), P(None, "mp")),
        out_specs=P("dp", "mp"),
        check_vma=False,
    )
```

```python
import functools

import jax
import jax.numpy as jnp
from jax import lax
from jax.experimental import pallas as pl
from jax.experimental.pallas import tpu as pltpu
from jax.sharding import PartitionSpec as P

TILE = 256
VMEM_BYTES = 44 * 1024 * 1024
MESH = pl.DeviceIdType.MESH


def dot(left, right, left_dim=1, right_dim=0):
    return lax.dot_general(
        left, right, (((left_dim,), (right_dim,)), ((), ())), preferred_element_type=jnp.float32
    )


def low(value):
    return value.astype(jnp.bfloat16)


def remote(source, target, send, recv, device):
    return pltpu.make_async_remote_copy(
        src_ref=source, dst_ref=target, send_sem=send, recv_sem=recv,
        device_id=device, device_id_type=MESH,
    )


def gram_kernel(
    n_dp, n_chips, f_ref, o_ref, all_ref, gram_ref,
    others, slab, sibling_half, out_half, chip_in,
    f_send, f_recv, o_send, o_recv, s_send, s_recv, z_send, z_recv,
    a_send, a_recv, b_send, b_recv, c_send, c_recv,
):
    tokens = f_ref.shape[0]
    half = tokens // 2
    piece = half // n_chips
    row = lax.axis_index("dp")
    owner = lax.axis_index("mp")
    chip = owner // 2
    core = owner % 2
    sibling = {"dp": row, "mp": chip * 2 + (1 - core)}
    rows = [{"dp": lax.rem(row + s, n_dp), "mp": owner} for s in range(1, n_dp)]
    chips = [{"dp": row, "mp": lax.rem(chip + s, n_chips) * 2 + core} for s in range(1, n_chips)]

    barrier = pltpu.get_barrier_semaphore()
    for device in rows + chips + [sibling]:
        pl.semaphore_signal(barrier, inc=1, device_id=device, device_id_type=MESH)
    pl.semaphore_wait(barrier, n_dp + n_chips - 1)

    f_copies = [
        remote(f_ref, others.at[s], f_send.at[s], f_recv.at[s], rows[s]) for s in range(n_dp - 1)
    ]
    own_tokens = pl.ds(pl.multiple_of(row * tokens, tokens), tokens)
    o_copies = [
        remote(o_ref, all_ref.at[own_tokens], o_send.at[s], o_recv.at[s], rows[s])
        for s in range(n_dp - 1)
    ]
    for copy in f_copies:
        copy.start()
    all_ref[own_tokens, :] = o_ref[...]

    slab[:, own_tokens] = dot(f_ref[...], f_ref[...], 1, 1)
    for s in range(n_dp - 1):
        source = lax.rem(row + n_dp - s - 1, n_dp)
        f_copies[s].wait_recv()
        slab[:, pl.ds(pl.multiple_of(source * tokens, tokens), tokens)] = dot(
            f_ref[...], others[s], 1, 1
        )

    for copy in o_copies:
        copy.start()

    theirs = pl.ds(pl.multiple_of((1 - core) * half, half), half)
    to_sibling = remote(slab.at[theirs], sibling_half, s_send, s_recv, sibling)
    to_sibling.start()
    to_sibling.wait_recv()
    mine = pl.multiple_of(core * half, half)
    out_half[...] = low(slab[pl.ds(mine, half), :] + sibling_half[...])

    z_copies = []
    for s in range(n_chips - 1):
        target = lax.rem(chip + s + 1, n_chips)
        z_copies.append(
            remote(
                out_half.at[pl.ds(pl.multiple_of(target * piece, piece), piece)],
                chip_in.at[s], z_send.at[s], z_recv.at[s], chips[s],
            )
        )
        z_copies[-1].start()
    offset = pl.multiple_of(chip * piece, piece)
    total = slab[pl.ds(pl.multiple_of(mine + offset, piece), piece), :] + sibling_half[pl.ds(offset, piece), :]
    for s in range(n_chips - 1):
        z_copies[s].wait_recv()
        total = total + chip_in[s].astype(jnp.float32)

    start = row * tokens + mine
    block = pl.ds(pl.multiple_of(start + offset, piece), piece)
    gram_ref[block, :] = low(total)
    a_copies = [
        remote(gram_ref.at[block], gram_ref.at[block], a_send.at[s], a_recv.at[s], chips[s])
        for s in range(n_chips - 1)
    ]
    for copy in a_copies:
        copy.start()
    for copy in a_copies:
        copy.wait_recv()

    strip = pl.ds(pl.multiple_of(start, half), half)
    b_copies = [
        remote(gram_ref.at[strip], gram_ref.at[strip], b_send.at[s], b_recv.at[s], rows[s])
        for s in range(n_dp - 1)
    ]
    for copy in b_copies:
        copy.start()
    c_copies = [remote(gram_ref.at[strip], gram_ref.at[strip], c_send.at[0], c_recv.at[0], sibling)]
    c_copies[0].start()
    for s in range(n_dp - 1):
        source = lax.rem(row + n_dp - s - 1, n_dp)
        b_copies[s].wait_recv()
        arrived = pl.ds(pl.multiple_of(source * tokens + mine, half), half)
        c_copies.append(
            remote(gram_ref.at[arrived], gram_ref.at[arrived], c_send.at[s + 1], c_recv.at[s + 1], sibling)
        )
        c_copies[-1].start()
    for copy in c_copies + o_copies:
        copy.wait_recv()
    for copy in f_copies + o_copies + [to_sibling] + z_copies + a_copies + b_copies + c_copies:
        copy.wait_send()


def gather_and_gram(features, out_grads, n_dp, n_mp):
    tokens, depth = features.shape
    every = n_dp * tokens
    n_chips = n_mp // 2
    half = tokens // 2
    dma = pltpu.SemaphoreType.DMA
    peers = [dma((n_dp - 1,))] * 2
    around = [dma((n_chips - 1,))] * 2
    whole = pl.BlockSpec(memory_space=pltpu.VMEM)
    return pl.pallas_call(
        functools.partial(gram_kernel, n_dp, n_chips),
        out_shape=[
            jax.ShapeDtypeStruct((every, out_grads.shape[1]), jnp.bfloat16),
            jax.ShapeDtypeStruct((every, every), jnp.bfloat16),
        ],
        in_specs=[whole, whole],
        out_specs=[whole, whole],
        scratch_shapes=[
            pltpu.VMEM((n_dp - 1, tokens, depth), jnp.bfloat16),
            pltpu.VMEM((tokens, every), jnp.float32),
            pltpu.VMEM((half, every), jnp.float32),
            pltpu.VMEM((half, every), jnp.bfloat16),
            pltpu.VMEM((n_chips - 1, half // n_chips, every), jnp.bfloat16),
        ]
        + peers + peers + [dma, dma] + around + around + peers + [dma((n_dp,))] * 2,
        compiler_params=pltpu.CompilerParams(
            collective_id=0, has_side_effects=True, vmem_limit_bytes=VMEM_BYTES
        ),
        cost_estimate=pl.CostEstimate(flops=2 * tokens * every * depth, bytes_accessed=200_000_000, transcendentals=0),
        name="gather_and_gram",
    )(features, out_grads)


def even_part(square):
    width = square.shape[0]
    half = low(square)
    second = dot(half, half)
    on_diagonal = lax.broadcasted_iota(jnp.int32, (width, width), 0) == lax.broadcasted_iota(
        jnp.int32, (width, width), 1
    )
    tail = jnp.where(on_diagonal, 0.375, 0.0) - 0.3125 * square + 0.0625 * second
    return low(-0.5 * square + dot(low(second), low(tail)))


def round_kernel(n_dp, n_mp, last, picked_ref, gram_ref, *refs):
    if last:
        (first_ref, second_ref, wide_ref, got_ref, staying_ref, arrived_ref, copy_ref, own_ref, *scratch) = refs
        shift = 0
    else:
        first_ref, wide_ref, staying_ref, arrived_ref, copy_ref, *scratch = refs
        second_ref = first_ref
        shift = first_ref.shape[1] // 2
    moving, cross, upper, lower, side, m_send, m_recv, x_send, x_recv = scratch
    tokens, width = staying_ref.shape
    row = lax.axis_index("dp")
    owner = lax.axis_index("mp")
    right = {"dp": row, "mp": lax.rem(owner + 1, n_mp)}
    left = {"dp": row, "mp": lax.rem(owner + n_mp - 1, n_mp)}
    greet = [right, left]
    per = wide_ref.shape[0] // n_dp
    rows = [{"dp": lax.rem(row + s, n_dp), "mp": owner} for s in range(1, n_dp)]
    if not last:
        greet = greet + rows

    barrier = pltpu.get_barrier_semaphore()
    for device in greet:
        pl.semaphore_signal(barrier, inc=1, device_id=device, device_id_type=MESH)
    pl.semaphore_wait(barrier, len(greet))

    if last:
        sibling = {"dp": row, "mp": owner + 1 - 2 * (owner % 2)}
        exchange = [
            remote(got_ref, copy_ref, x_send.at[0], x_recv.at[0], sibling),
            remote(wide_ref.at[pl.ds(row * per, per)], own_ref, x_send.at[1], x_recv.at[1], sibling),
        ]
    else:
        exchange = [
            remote(
                wide_ref.at[pl.ds(lax.rem(row + s + 1, n_dp) * per, per)], copy_ref.at[s],
                x_send.at[s], x_recv.at[s], rows[s],
            )
            for s in range(n_dp - 1)
        ]
    for copy in exchange:
        copy.start()

    cross[...] = jnp.zeros_like(cross)

    @pl.loop(0, tokens // TILE)
    def _(step):
        tile = pl.ds(pl.multiple_of(step * TILE, TILE), TILE)
        product = low(dot(gram_ref[tile, :], second_ref[:, shift : shift + width]))
        cross[...] += dot(first_ref[tile, :width], product, 0, 0)

    value = cross[...]
    scale = 0.5 * lax.rsqrt(jnp.sum(value * value) + 1e-06)
    angle = low(scale * value)
    upper[...] = even_part(dot(angle, angle, 1, 1))
    lower[...] = even_part(dot(angle, angle, 0, 0))
    side[...] = low(angle.astype(jnp.float32) + dot(upper[...], angle))
    keep = picked_ref[0] == 0

    travel = []
    for step in range(tokens // TILE):
        tile = pl.ds(step * TILE, TILE)
        first = first_ref[tile, :width]
        second = second_ref[tile, shift : shift + width]
        new_first = low(first.astype(jnp.float32) + (dot(first, upper[...]) - dot(second, side[...], 1, 1)))
        new_second = low(second.astype(jnp.float32) + (dot(first, side[...]) + dot(second, lower[...])))
        moving[tile, :] = jnp.where(keep, new_second, new_first)
        travel.append(remote(moving.at[tile], arrived_ref.at[tile], m_send.at[step], m_recv.at[step], right))
        travel[-1].start()
        staying_ref[tile, :] = jnp.where(keep, new_first, new_second)
    for copy in travel + exchange:
        copy.wait_recv()
    for copy in travel + exchange:
        copy.wait_send()


def one_round(n_dp, n_mp, last, picked, gram, blocks, features):
    tokens = gram.shape[0]
    width = blocks[0].shape[1] // (1 if last else 2)
    per = features[0].shape[0] // n_dp
    depth = features[0].shape[1:]
    tiles = tokens // TILE
    block = jax.ShapeDtypeStruct((tokens, width), jnp.bfloat16)
    moved = [jax.ShapeDtypeStruct((n_dp - 1, per) + depth, jnp.bfloat16)]
    if last:
        moved.append(jax.ShapeDtypeStruct((per,) + depth, jnp.bfloat16))
    copies = 2 if last else n_dp - 1
    vmem = pl.BlockSpec(memory_space=pltpu.VMEM)
    there = pl.BlockSpec(memory_space=pl.ANY)
    square = pltpu.VMEM((width, width), jnp.bfloat16)
    dma = pltpu.SemaphoreType.DMA
    return pl.pallas_call(
        functools.partial(round_kernel, n_dp, n_mp, last),
        out_shape=[block, block] + moved,
        in_specs=[pl.BlockSpec(memory_space=pltpu.SMEM), vmem] + [vmem] * len(blocks) + [there] * len(features),
        out_specs=[vmem, vmem] + [there] * len(moved),
        scratch_shapes=[
            pltpu.VMEM((tokens, width), jnp.bfloat16),
            pltpu.VMEM((width, width), jnp.float32),
            square, square, square,
            dma((tiles,)), dma((tiles,)), dma((copies,)), dma((copies,)),
        ],
        compiler_params=pltpu.CompilerParams(
            collective_id=2 if last else 1, has_side_effects=True, vmem_limit_bytes=VMEM_BYTES
        ),
        cost_estimate=pl.CostEstimate(
            flops=2 * tokens * width * (tokens + 5 * width) + 14 * width**3,
            bytes_accessed=2 * tokens * (tokens + 4 * width), transcendentals=1,
        ),
        name="jacobi_round_last" if last else "jacobi_round",
    )(picked, gram, *blocks, *features)


def product_kernel(n_dp, tokens, *refs):
    both = (refs[:n_dp], refs[n_dp : 2 * n_dp])
    staying_ref, arrived_ref, out_ref = refs[2 * n_dp :]
    row = lax.axis_index("dp")
    core = lax.axis_index("mp") % 2
    width = staying_ref.shape[1]
    for place, parts in enumerate(both):
        where = core if place == 0 else 1 - core
        for side, block in enumerate((staying_ref, arrived_ref)):
            total = None
            for s in range(n_dp):
                source = lax.rem(row + n_dp - s, n_dp)
                features = parts[s][...]
                features = features.reshape(features.shape[-2:])
                term = dot(features, block[pl.ds(pl.multiple_of(source * tokens, tokens), tokens), :], 0, 0)
                total = term if total is None else total + term
            out_ref[0, where, :, side * width : (side + 1) * width] = low(total)


def final_product(mine, got, theirs, got_theirs, staying, arrived):
    n_dp = got.shape[0] + 1
    groups, tokens, depth = mine.shape
    tile = min(TILE, depth)
    per = depth // tile
    width = staying.shape[1]
    full = pl.BlockSpec(staying.shape, lambda i: (0, 0))
    own = pl.BlockSpec((1, tokens, tile), lambda i: (i // per, 0, i % per))

    def other(s):
        return pl.BlockSpec((1, 1, tokens, tile), lambda i: (s, i // per, 0, i % per))

    others = [other(s) for s in range(n_dp - 1)]
    out = pl.pallas_call(
        functools.partial(product_kernel, n_dp, tokens),
        grid=(groups * per,),
        out_shape=jax.ShapeDtypeStruct((groups, 2, depth, 2 * width), jnp.bfloat16),
        in_specs=([own] + others) * 2 + [full, full],
        out_specs=pl.BlockSpec((1, 2, tile, 2 * width), lambda i: (i // per, 0, i % per, 0)),
        compiler_params=pltpu.CompilerParams(vmem_limit_bytes=VMEM_BYTES),
        cost_estimate=pl.CostEstimate(
            flops=8 * groups * depth * width * tokens * n_dp,
            bytes_accessed=4 * groups * depth * (n_dp * tokens + 2 * width), transcendentals=0,
        ),
        name="final_product",
    )(mine, *[got] * (n_dp - 1), theirs, *[got_theirs] * (n_dp - 1), staying, arrived)
    return out.reshape(groups * 2 * depth, 2 * width)


def on_device(features, out_grads, matching):
    n_dp = lax.axis_size("dp")
    n_mp = lax.axis_size("mp")
    groups = n_mp // 2 // n_dp
    same_core = [list(range(core, n_mp, 2)) for core in range(2)]
    wide = lax.all_gather(features, "mp", axis=0, axis_index_groups=same_core)
    joined, gram = gather_and_gram(features, out_grads, n_dp, n_mp)
    staying, arrived, got = one_round(n_dp, n_mp, False, matching[0], gram, [joined], [wide])
    staying, arrived, got_theirs, theirs = one_round(
        n_dp, n_mp, True, matching[1], gram, [staying, arrived], [wide, got]
    )
    mine = lax.dynamic_slice_in_dim(wide, lax.axis_index("dp") * groups, groups, axis=0)
    return final_product(mine, got, theirs, got_theirs, staying, arrived)


def solution(mesh):
    return jax.shard_map(
        on_device,
        mesh=mesh,
        in_specs=(P("dp", "mp"), P("dp", "mp"), P(None, "mp")),
        out_specs=P("dp", "mp"),
        check_vma=False,
    )
```

```python
import functools

import jax
import jax.numpy as jnp
from jax import lax
from jax.experimental import pallas as pl
from jax.experimental.pallas import tpu as pltpu
from jax.sharding import PartitionSpec as P

TILE = 256
VMEM_BYTES = 44 * 1024 * 1024
MESH = pl.DeviceIdType.MESH


def dot(left, right, left_dim=1, right_dim=0):
    return lax.dot_general(
        left, right, (((left_dim,), (right_dim,)), ((), ())), preferred_element_type=jnp.float32
    )


def low(value):
    return value.astype(jnp.bfloat16)


def remote(source, target, send, recv, device):
    return pltpu.make_async_remote_copy(
        src_ref=source, dst_ref=target, send_sem=send, recv_sem=recv,
        device_id=device, device_id_type=MESH,
    )


def gram_kernel(
    n_dp, n_chips, picked_ref, f_ref, o_ref, staying_ref, arrived_ref, gram_ref,
    all_ref, others, slab, sibling_half, out_half, chip_in,
    f_send, f_recv, o_send, o_recv, s_send, s_recv, z_send, z_recv,
    a_send, a_recv, b_send, b_recv, c_send, c_recv, *scratch,
):
    tokens = f_ref.shape[0]
    half = tokens // 2
    piece = half // n_chips
    row = lax.axis_index("dp")
    owner = lax.axis_index("mp")
    chip = owner // 2
    core = owner % 2
    sibling = {"dp": row, "mp": chip * 2 + (1 - core)}
    rows = [{"dp": lax.rem(row + s, n_dp), "mp": owner} for s in range(1, n_dp)]
    chips = [{"dp": row, "mp": lax.rem(chip + s, n_chips) * 2 + core} for s in range(1, n_chips)]

    barrier = pltpu.get_barrier_semaphore()
    right = {"dp": row, "mp": lax.rem(owner + 1, 2 * n_chips)}
    left = {"dp": row, "mp": lax.rem(owner + 2 * n_chips - 1, 2 * n_chips)}
    for device in rows + chips + [right, left]:
        pl.semaphore_signal(barrier, inc=1, device_id=device, device_id_type=MESH)
    pl.semaphore_wait(barrier, n_dp + n_chips)

    f_copies = [
        remote(f_ref, others.at[s], f_send.at[s], f_recv.at[s], rows[s]) for s in range(n_dp - 1)
    ]
    own_tokens = pl.ds(pl.multiple_of(row * tokens, tokens), tokens)
    o_copies = [
        remote(o_ref, all_ref.at[own_tokens], o_send.at[s], o_recv.at[s], rows[s])
        for s in range(n_dp - 1)
    ]
    for copy in f_copies:
        copy.start()
    all_ref[own_tokens, :] = o_ref[...]

    slab[:, own_tokens] = dot(f_ref[...], f_ref[...], 1, 1)
    for s in range(n_dp - 1):
        source = lax.rem(row + n_dp - s - 1, n_dp)
        f_copies[s].wait_recv()
        slab[:, pl.ds(pl.multiple_of(source * tokens, tokens), tokens)] = dot(
            f_ref[...], others[s], 1, 1
        )

    for copy in o_copies:
        copy.start()

    theirs = pl.ds(pl.multiple_of((1 - core) * half, half), half)
    to_sibling = remote(slab.at[theirs], sibling_half, s_send, s_recv, sibling)
    to_sibling.start()
    to_sibling.wait_recv()
    mine = pl.multiple_of(core * half, half)
    out_half[...] = low(slab[pl.ds(mine, half), :] + sibling_half[...])

    z_copies = []
    for s in range(n_chips - 1):
        target = lax.rem(chip + s + 1, n_chips)
        z_copies.append(
            remote(
                out_half.at[pl.ds(pl.multiple_of(target * piece, piece), piece)],
                chip_in.at[s], z_send.at[s], z_recv.at[s], chips[s],
            )
        )
        z_copies[-1].start()
    offset = pl.multiple_of(chip * piece, piece)
    total = slab[pl.ds(pl.multiple_of(mine + offset, piece), piece), :] + sibling_half[pl.ds(offset, piece), :]
    for s in range(n_chips - 1):
        z_copies[s].wait_recv()
        total = total + chip_in[s].astype(jnp.float32)

    start = row * tokens + mine
    block = pl.ds(pl.multiple_of(start + offset, piece), piece)
    gram_ref[block, :] = low(total)
    a_copies = [
        remote(gram_ref.at[block], gram_ref.at[block], a_send.at[s], a_recv.at[s], chips[s])
        for s in range(n_chips - 1)
    ]
    for copy in a_copies:
        copy.start()
    for copy in a_copies:
        copy.wait_recv()

    strip = pl.ds(pl.multiple_of(start, half), half)
    b_copies = [
        remote(gram_ref.at[strip], gram_ref.at[strip], b_send.at[s], b_recv.at[s], rows[s])
        for s in range(n_dp - 1)
    ]
    for copy in b_copies:
        copy.start()
    c_copies = [remote(gram_ref.at[strip], gram_ref.at[strip], c_send.at[0], c_recv.at[0], sibling)]
    c_copies[0].start()
    for s in range(n_dp - 1):
        source = lax.rem(row + n_dp - s - 1, n_dp)
        b_copies[s].wait_recv()
        arrived = pl.ds(pl.multiple_of(source * tokens + mine, half), half)
        c_copies.append(
            remote(gram_ref.at[arrived], gram_ref.at[arrived], c_send.at[s + 1], c_recv.at[s + 1], sibling)
        )
        c_copies[-1].start()
    for copy in c_copies + o_copies:
        copy.wait_recv()
    travel = jacobi_round(
        picked_ref, gram_ref, all_ref, all_ref, all_ref.shape[1] // 2, staying_ref, arrived_ref, right, *scratch
    )
    for copy in travel:
        copy.wait_recv()
    for copy in f_copies + o_copies + [to_sibling] + z_copies + a_copies + b_copies + c_copies + travel:
        copy.wait_send()


def round_scratch(every, width):
    square = pltpu.VMEM((width, width), jnp.bfloat16)
    tiles = pltpu.SemaphoreType.DMA((every // TILE,))
    return [
        pltpu.VMEM((every, width), jnp.bfloat16), pltpu.VMEM((width, width), jnp.float32),
        square, square, square, tiles, tiles,
    ]


def gather_and_round(picked, features, out_grads, n_dp, n_mp):
    tokens, depth = features.shape
    every = n_dp * tokens
    n_chips = n_mp // 2
    half = tokens // 2
    width = out_grads.shape[1] // 2
    dma = pltpu.SemaphoreType.DMA
    peers = [dma((n_dp - 1,))] * 2
    around = [dma((n_chips - 1,))] * 2
    whole = pl.BlockSpec(memory_space=pltpu.VMEM)
    block = jax.ShapeDtypeStruct((every, width), jnp.bfloat16)
    return pl.pallas_call(
        functools.partial(gram_kernel, n_dp, n_chips),
        out_shape=[block, block, jax.ShapeDtypeStruct((every, every), jnp.bfloat16)],
        in_specs=[pl.BlockSpec(memory_space=pltpu.SMEM), whole, whole],
        out_specs=[whole, whole, whole],
        scratch_shapes=[
            pltpu.VMEM((every, 2 * width), jnp.bfloat16),
            pltpu.VMEM((n_dp - 1, tokens, depth), jnp.bfloat16),
            pltpu.VMEM((tokens, every), jnp.float32),
            pltpu.VMEM((half, every), jnp.float32),
            pltpu.VMEM((half, every), jnp.bfloat16),
            pltpu.VMEM((n_chips - 1, half // n_chips, every), jnp.bfloat16),
        ]
        + peers + peers + [dma, dma] + around + around + peers + [dma((n_dp,))] * 2
        + round_scratch(every, width),
        compiler_params=pltpu.CompilerParams(
            collective_id=0, has_side_effects=True, vmem_limit_bytes=VMEM_BYTES
        ),
        cost_estimate=pl.CostEstimate(
            flops=2 * tokens * every * depth, bytes_accessed=250_000_000, transcendentals=0
        ),
        name="gather_and_round",
    )(picked, features, out_grads)


def even_part(square):
    width = square.shape[0]
    half = low(square)
    second = dot(half, half)
    on_diagonal = lax.broadcasted_iota(jnp.int32, (width, width), 0) == lax.broadcasted_iota(
        jnp.int32, (width, width), 1
    )
    tail = jnp.where(on_diagonal, 0.375, 0.0) - 0.3125 * square + 0.0625 * second
    return low(-0.5 * square + dot(low(second), low(tail)))


def jacobi_round(
    picked_ref, gram_ref, first_ref, second_ref, shift, staying_ref, arrived_ref, right,
    moving, cross, upper, lower, side, m_send, m_recv,
):
    tokens, width = staying_ref.shape
    cross[...] = jnp.zeros_like(cross)

    @pl.loop(0, tokens // TILE)
    def _(step):
        tile = pl.ds(pl.multiple_of(step * TILE, TILE), TILE)
        product = low(dot(gram_ref[tile, :], second_ref[:, shift : shift + width]))
        cross[...] += dot(first_ref[tile, :width], product, 0, 0)

    value = cross[...]
    scale = 0.5 * lax.rsqrt(jnp.sum(value * value) + 1e-06)
    angle = low(scale * value)
    upper[...] = even_part(dot(angle, angle, 1, 1))
    lower[...] = even_part(dot(angle, angle, 0, 0))
    side[...] = low(angle.astype(jnp.float32) + dot(upper[...], angle))
    keep = picked_ref[0] == 0

    travel = []
    for step in range(tokens // TILE):
        tile = pl.ds(step * TILE, TILE)
        first = first_ref[tile, :width]
        second = second_ref[tile, shift : shift + width]
        new_first = low(first.astype(jnp.float32) + (dot(first, upper[...]) - dot(second, side[...], 1, 1)))
        new_second = low(second.astype(jnp.float32) + (dot(first, side[...]) + dot(second, lower[...])))
        moving[tile, :] = jnp.where(keep, new_second, new_first)
        travel.append(remote(moving.at[tile], arrived_ref.at[tile], m_send.at[step], m_recv.at[step], right))
        travel[-1].start()
        staying_ref[tile, :] = jnp.where(keep, new_first, new_second)
    return travel


def last_kernel(
    n_dp, n_mp, picked_ref, gram_ref, first_ref, second_ref, wide_ref,
    staying_ref, arrived_ref, got_ref, got_theirs_ref, theirs_ref,
    x_send, x_recv, y_send, y_recv, *scratch,
):
    row = lax.axis_index("dp")
    owner = lax.axis_index("mp")
    right = {"dp": row, "mp": lax.rem(owner + 1, n_mp)}
    left = {"dp": row, "mp": lax.rem(owner + n_mp - 1, n_mp)}
    sibling = {"dp": row, "mp": owner + 1 - 2 * (owner % 2)}
    per = wide_ref.shape[0] // n_dp
    rows = [{"dp": lax.rem(row + s, n_dp), "mp": owner} for s in range(1, n_dp)]

    barrier = pltpu.get_barrier_semaphore()
    for device in [right, left] + rows:
        pl.semaphore_signal(barrier, inc=1, device_id=device, device_id_type=MESH)
    pl.semaphore_wait(barrier, n_dp + 1)

    exchange = [
        remote(
            wide_ref.at[pl.ds(lax.rem(row + s + 1, n_dp) * per, per)], got_ref.at[s],
            x_send.at[s], x_recv.at[s], rows[s],
        )
        for s in range(n_dp - 1)
    ]
    across = [
        remote(wide_ref.at[pl.ds(row * per, per)], theirs_ref, y_send.at[n_dp - 1], y_recv.at[n_dp - 1], sibling)
    ]
    for copy in exchange + across:
        copy.start()
    travel = jacobi_round(
        picked_ref, gram_ref, first_ref, second_ref, 0, staying_ref, arrived_ref, right, *scratch
    )
    for s in range(n_dp - 1):
        exchange[s].wait_recv()
        across.append(remote(got_ref.at[s], got_theirs_ref.at[s], y_send.at[s], y_recv.at[s], sibling))
        across[-1].start()
    for copy in travel + across:
        copy.wait_recv()
    for copy in travel + exchange + across:
        copy.wait_send()


def last_round(n_dp, n_mp, picked, gram, first, second, wide):
    every, width = first.shape
    per = wide.shape[0] // n_dp
    depth = wide.shape[1:]
    block = jax.ShapeDtypeStruct((every, width), jnp.bfloat16)
    moved = jax.ShapeDtypeStruct((n_dp - 1, per) + depth, jnp.bfloat16)
    vmem = pl.BlockSpec(memory_space=pltpu.VMEM)
    there = pl.BlockSpec(memory_space=pl.ANY)
    dma = pltpu.SemaphoreType.DMA
    return pl.pallas_call(
        functools.partial(last_kernel, n_dp, n_mp),
        out_shape=[block, block, moved, moved, jax.ShapeDtypeStruct((per,) + depth, jnp.bfloat16)],
        in_specs=[pl.BlockSpec(memory_space=pltpu.SMEM), vmem, vmem, vmem, there],
        out_specs=[vmem, vmem, there, there, there],
        scratch_shapes=[dma((n_dp - 1,)), dma((n_dp - 1,)), dma((n_dp,)), dma((n_dp,))]
        + round_scratch(every, width),
        compiler_params=pltpu.CompilerParams(
            collective_id=1, has_side_effects=True, vmem_limit_bytes=VMEM_BYTES
        ),
        cost_estimate=pl.CostEstimate(
            flops=2 * every * width * (every + 5 * width) + 14 * width**3,
            bytes_accessed=2 * every * (every + 4 * width), transcendentals=1,
        ),
        name="last_round",
    )(picked, gram, first, second, wide)


def product_kernel(n_dp, tokens, *refs):
    both = (refs[:n_dp], refs[n_dp : 2 * n_dp])
    staying_ref, arrived_ref, out_ref = refs[2 * n_dp :]
    row = lax.axis_index("dp")
    core = lax.axis_index("mp") % 2
    width = staying_ref.shape[1]
    for place, parts in enumerate(both):
        where = core if place == 0 else 1 - core
        for side, block in enumerate((staying_ref, arrived_ref)):
            total = None
            for s in range(n_dp):
                source = lax.rem(row + n_dp - s, n_dp)
                features = parts[s][...]
                features = features.reshape(features.shape[-2:])
                term = dot(features, block[pl.ds(pl.multiple_of(source * tokens, tokens), tokens), :], 0, 0)
                total = term if total is None else total + term
            out_ref[0, where, :, side * width : (side + 1) * width] = low(total)


def final_product(mine, got, theirs, got_theirs, staying, arrived):
    n_dp = got.shape[0] + 1
    groups, tokens, depth = mine.shape
    tile = min(TILE, depth)
    per = depth // tile
    width = staying.shape[1]
    full = pl.BlockSpec(staying.shape, lambda i: (0, 0))
    own = pl.BlockSpec((1, tokens, tile), lambda i: (i // per, 0, i % per))

    def other(s):
        return pl.BlockSpec((1, 1, tokens, tile), lambda i: (s, i // per, 0, i % per))

    others = [other(s) for s in range(n_dp - 1)]
    out = pl.pallas_call(
        functools.partial(product_kernel, n_dp, tokens),
        grid=(groups * per,),
        out_shape=jax.ShapeDtypeStruct((groups, 2, depth, 2 * width), jnp.bfloat16),
        in_specs=([own] + others) * 2 + [full, full],
        out_specs=pl.BlockSpec((1, 2, tile, 2 * width), lambda i: (i // per, 0, i % per, 0)),
        compiler_params=pltpu.CompilerParams(vmem_limit_bytes=VMEM_BYTES),
        cost_estimate=pl.CostEstimate(
            flops=8 * groups * depth * width * tokens * n_dp,
            bytes_accessed=4 * groups * depth * (n_dp * tokens + 2 * width), transcendentals=0,
        ),
        name="final_product",
    )(mine, *[got] * (n_dp - 1), theirs, *[got_theirs] * (n_dp - 1), staying, arrived)
    return out.reshape(groups * 2 * depth, 2 * width)


def on_device(features, out_grads, matching):
    n_dp = lax.axis_size("dp")
    n_mp = lax.axis_size("mp")
    groups = n_mp // 2 // n_dp
    same_core = [list(range(core, n_mp, 2)) for core in range(2)]
    wide = lax.all_gather(features, "mp", axis=0, axis_index_groups=same_core)
    staying, arrived, gram = gather_and_round(matching[0], features, out_grads, n_dp, n_mp)
    staying, arrived, got, got_theirs, theirs = last_round(
        n_dp, n_mp, matching[1], gram, staying, arrived, wide
    )
    mine = lax.dynamic_slice_in_dim(wide, lax.axis_index("dp") * groups, groups, axis=0)
    return final_product(mine, got, theirs, got_theirs, staying, arrived)


def solution(mesh):
    return jax.shard_map(
        on_device,
        mesh=mesh,
        in_specs=(P("dp", "mp"), P("dp", "mp"), P(None, "mp")),
        out_specs=P("dp", "mp"),
        check_vma=False,
    )
```
